32 devices in a mesh: groups: 2 (over y), gy: 4 (over z), gz: 2 (over x), gx: 2 (over core).
Axes of the slice: x: 2, y: 2, z: 4, core: 2. Of those that a mesh axis runs over, the one named last changes fastest.
Arguments:
- block_input: bfloat16 [12, 4, 72, 768], P(None, 'gz', ('groups', 'gy'), 'gx'), parts along dimension 2, may hold values from -6 to 6
- first_pre: bfloat16 [12, 4, 72, 768], P(None, 'gz', ('groups', 'gy'), 'gx'), parts along dimension 2, may hold values from -6 to 6
- second_pre: bfloat16 [60, 4, 24, 256], P(None, 'gz', ('groups', 'gy'), 'gx'), parts along dimension 2, may hold values from -6 to 6
- output_cotangent: bfloat16 [60, 4, 24, 256], P(None, 'gz', ('groups', 'gy'), 'gx'), parts along dimension 2, may hold values from -6 to 6
- first_kernel: bfloat16 [3, 3, 3, 12, 12], replicated, may hold values from -0.3125 to 0.3125
- second_kernel: bfloat16 [3, 3, 60, 12], replicated, may hold values from -0.625 to 0.625
- third_kernel: bfloat16 [3, 3, 60, 60], replicated, may hold values from -0.25 to 0.25
Outputs:
- block_gradient: bfloat16 [12, 4, 72, 768], P(None, 'gz', ('groups', 'gy'), 'gx'), parts along dimension 2
- first_gradient: float32 [6, 3, 3, 12, 12], P('groups'), parts along dimension 0
- second_gradient: float32 [6, 3, 60, 12], P('groups'), parts along dimension 0
- third_gradient: float32 [6, 3, 60, 60], P('groups'), parts along dimension 0
The draws below stay inside these ranges and needn't reach their ends.
There are 2 independent parts, one for each index of `groups`. The reference program is written for one: setup_inputs(seed, part) draws one part's arguments, and reference() takes and returns one part's arrays. A program takes and returns all parts, laid end to end along the dimension named above; an argument that names none is the same for every part. Nothing has to cross between parts.
All inputs are finite; a program needn't handle non-finite values.
Results may differ from the reference program's by a relative error of at most 0.0057.
Values may be sent and summed in bfloat16 or wider, within the bound.
A program may use at most 64 MiB of HBM per device.

```python
import math
import jax
import jax.numpy as jnp
from jax import lax

C0 = 12
C1 = 60
NZ = 4
NY = 36
NX = 768
MY = 12
MX = 256


def levels(own_key, extent, shards, low, top_value):
    loudness, own = 1.0, jax.random.fold_in(own_key, 6)
    for axis_at, blocks in shards:
        steps = jnp.exp(jax.random.uniform(jax.random.fold_in(own, axis_at), (blocks,), jnp.float32, low / len(shards), top_value / len(shards)))
        loudness = loudness * jnp.repeat(steps, extent[axis_at] // blocks).reshape([-1 if axis == axis_at else 1 for axis in range(len(extent))])
    return loudness


def scatter_about(rng, extent, deviation, bound, pieces=(), kind=jnp.bfloat16):
    loudness = levels(rng, extent, pieces, -0.22, 0.18) if pieces else 1.0
    values = jax.random.normal(rng, extent, jnp.float32) * deviation * loudness
    return jnp.minimum(jnp.maximum(values, -bound), bound).astype(kind)


def setup_inputs(seed: int = 0, part: int = 0) -> dict:
    splits = jax.random.split(jax.random.key(seed), 8)
    part_splits = jax.random.split(jax.random.fold_in(splits[7], part), 8)
    return {
        "block_input": scatter_about(part_splits[0], (C0, NZ, NY, NX), 1.0, 6.0, ((1, 2), (2, 4), (3, 2))),
        "first_pre": scatter_about(part_splits[1], (C0, NZ, NY, NX), 1.0, 6.0, ((1, 2), (2, 4), (3, 2))),
        "second_pre": scatter_about(part_splits[2], (C1, NZ, MY, MX), 1.0, 6.0, ((1, 2), (2, 4), (3, 2))),
        "output_cotangent": scatter_about(part_splits[3], (C1, NZ, MY, MX), 1.0, 6.0, ((1, 2), (2, 4), (3, 2))),
        "first_kernel": scatter_about(splits[4], (3, 3, 3, C0, C0), (27 * C0) ** -0.5, 0.3125),
        "second_kernel": scatter_about(splits[5], (3, 3, C1, C0), (9 * C0) ** -0.5, 0.625),
        "third_kernel": scatter_about(splits[6], (3, 3, C1, C1), (9 * C1) ** -0.5, 0.25),
    }


def widen(array, depth, width):
    return jnp.pad(array, ((0, 0), (depth, depth), (width, width), (width, width)))

def pool_max(activation):
    chans, sections, rows, columns = activation.shape
    windows = activation.reshape(chans, sections, rows // 3, 3, columns // 3, 3)
    return lax.optimization_barrier(jnp.max(windows, axis=(3, 5)))

def unpool(activation, coarse_values):
    chans, sections, rows, columns = activation.shape
    windows = activation.reshape(chans, sections, rows // 3, 3, columns // 3, 3)
    highest = lax.optimization_barrier(jnp.max(windows, axis=(3, 5)))
    claimed = jnp.zeros(highest.shape, dtype=bool)
    stacked_rows = []
    for a in range(3):
        columns_out = []
        for b in range(3):
            candidate = windows[:, :, :, a, :, b]
            winner = (candidate == highest) & jnp.logical_not(claimed)
            claimed = claimed | winner
            columns_out.append(jnp.where(winner, coarse_values, jnp.zeros_like(coarse_values)))
        stacked_rows.append(jnp.stack(columns_out, axis=4))
    return jnp.stack(stacked_rows, axis=3).reshape(chans, sections, rows, columns)

def transpose_conv(padded, kernel):
    flipped = jnp.flip(kernel, axis=(0, 1, 2)).transpose(4, 3, 0, 1, 2).astype(jnp.float32)
    result = lax.conv_general_dilated(padded[None].astype(jnp.float32), flipped, (1, 1, 1), 'VALID', dimension_numbers=('NCDHW', 'OIDHW', 'NCDHW'), precision=lax.Precision.HIGHEST)
    return result[0]

def kernel_grad(padded, activation, starts):
    result = lax.conv_general_dilated(padded[:, None].astype(jnp.float32), activation[:, None].astype(jnp.float32), (1, 1, 1), 'VALID', dimension_numbers=('NCDHW', 'OIDHW', 'NCDHW'), precision=lax.Precision.HIGHEST)
    for axis_pos, start in zip((2, 3, 4), starts):
        if start is not None:
            result = jnp.flip(lax.slice_in_dim(result, start - 2, start + 1, axis=axis_pos), axis=axis_pos)
    return result.transpose(2, 3, 4, 0, 1)

def reference(block_input, first_pre, second_pre, output_cotangent, first_kernel, second_kernel, third_kernel):
    first_relu = jnp.maximum(first_pre, jnp.zeros_like(first_pre))
    second_relu = jnp.maximum(second_pre, jnp.zeros_like(second_pre))
    pooled = pool_max(first_relu)
    coarse_scale = math.sqrt(NZ * MY * MX)
    fine_scale = math.sqrt(NZ * NY * NX)
    cot_padded = widen(output_cotangent, 0, 1)
    third_back = transpose_conv(cot_padded, third_kernel[None])
    coarse_delta = jnp.where(second_pre > 0, third_back, 0.0).astype(jnp.bfloat16)
    third_gradient = kernel_grad(cot_padded, second_relu, (None, 2, 2))[0] / coarse_scale
    delta_padded = widen(coarse_delta, 0, 1)
    pooled_back = transpose_conv(delta_padded, second_kernel[None])
    second_gradient = kernel_grad(delta_padded, pooled, (None, 2, 2))[0] / coarse_scale
    routed = unpool(first_relu, pooled_back)
    fine_delta = jnp.where(first_pre > 0, routed, 0.0).astype(jnp.bfloat16)
    fine_padded = widen(fine_delta, 1, 1)
    block_gradient = transpose_conv(fine_padded, first_kernel).astype(jnp.bfloat16)
    first_gradient = kernel_grad(fine_padded, block_input, (2, 2, 2)) / fine_scale
    return (block_gradient, first_gradient.astype(jnp.float32), second_gradient.astype(jnp.float32), third_gradient.astype(jnp.float32))
```

```python
import functools
import math

import jax
import jax.numpy as jnp
import numpy as np
from jax import lax
from jax.experimental import pallas as pl
from jax.experimental.pallas import tpu as pltpu
from jax.sharding import PartitionSpec as P

MESH = pl.DeviceIdType.MESH
F32, BF16 = jnp.float32, jnp.bfloat16


def dot(a, b, da, db):
    return lax.dot_general(a, b, (((da,), (db,)), ((), ())), preferred_element_type=F32)


def neighbour_moves(sections):
    return [(z, y, s) for z in sections for y in (-1, 0, 1) for s in (0, 1) if (z, y, s) != (0, 0, 0)]


COARSE = neighbour_moves((0,))
FINE = neighbour_moves((-1, 0, 1))


def kernel(
    ny, nz, rows,
    bi_ref, fp_ref, sp_ref, oc_ref, w1_ref, w2_ref, w3_ref, pick_ref, back_ref,
    out_ref, total_ref,
    cot, delta, fine, col, ext, split, lanes, gather, grad, inbox,
    cot_s, cot_r, delta_s, delta_r, fine_s, fine_r, sum_s, sum_r, all_s, all_r,
):
    gy, gz, gx = lax.axis_index("gy"), lax.axis_index("gz"), lax.axis_index("gx")

    def there(z, y):
        ok = None
        for at, step, size in ((gz, z, nz), (gy, y, ny)):
            if step:
                one = at < size - 1 if step > 0 else at > 0
                ok = one if ok is None else jnp.logical_and(ok, one)
        return ok

    def guarded(z, y, run):
        ok = there(z, y)
        if ok is None:
            run()
        else:
            pl.when(ok)(run)

    def device(z, y, s):
        return {"gz": gz + z, "gy": gy + y, "gx": 1 - gx if s else gx}

    cot[...] = jnp.zeros_like(cot)
    delta[...] = jnp.zeros_like(delta)
    fine[...] = jnp.zeros_like(fine)
    for z in range(2):
        for y in range(3):
            cot[0, z, y + 1] = oc_ref[z, y]

    barrier = pltpu.get_barrier_semaphore()
    count = jnp.int32(0)
    for z, y, s in FINE:
        def greet(z=z, y=y, s=s):
            pl.semaphore_signal(barrier, inc=1, device_id=device(z, y, s), device_id_type=MESH)
        guarded(z, y, greet)
        ok = there(z, y)
        count = count + (1 if ok is None else ok.astype(jnp.int32))
    for j in range(1, nz):
        pl.semaphore_signal(barrier, inc=1, device_id={"gz": lax.rem(gz + j, nz)}, device_id_type=MESH)
    for j in range(1, ny):
        pl.semaphore_signal(barrier, inc=1, device_id={"gy": lax.rem(gy + j, ny)}, device_id_type=MESH)
    pl.semaphore_wait(barrier, count + (nz - 1) + (ny - 1))

    def halo_copy(buf, send, recv, moves, m, arriving=False):
        z, y, s = moves[m]
        zs = slice(0, 2) if buf.shape[1] == 2 else slice(1, 3)
        zd = zs
        if z:
            zs, zd = (slice(2, 3), slice(0, 1)) if z > 0 else (slice(1, 2), slice(3, 4))
        ys = yd = slice(1, 4)
        if y:
            ys, yd = (slice(3, 4), slice(0, 1)) if y > 0 else (slice(1, 2), slice(4, 5))
        return pltpu.make_async_remote_copy(
            src_ref=buf.at[0, zs, ys], dst_ref=buf.at[s, zd, yd],
            send_sem=send.at[m], recv_sem=recv.at[m],
            device_id=device(z, y, s), device_id_type=MESH,
        )

    def start_halo(buf, send, recv, moves):
        for m, (z, y, s) in enumerate(moves):
            guarded(z, y, lambda m=m: halo_copy(buf, send, recv, moves, m).start())

    def wait_halo(buf, send, recv, moves):
        for m, (z, y, s) in enumerate(moves):
            guarded(-z, -y, lambda m=m: halo_copy(buf, send, recv, moves, m).wait_recv())

    def wait_sent(buf, send, recv, moves):
        for m, (z, y, s) in enumerate(moves):
            guarded(z, y, lambda m=m: halo_copy(buf, send, recv, moves, m).wait_send())

    def shifted(own, other):
        own, other = own.astype(F32), other.astype(F32)
        lane = lax.broadcasted_iota(jnp.int32, own.shape, 1)
        left = jnp.where(gx == 1, other, 0.0)
        right = jnp.where(gx == 0, other, 0.0)
        before = pltpu.roll(jnp.where(lane == 127, left, own), 1, 1)
        after = pltpu.roll(jnp.where(lane == 0, right, own), 127, 1)
        return before, after

    def columns(buf):
        for z in range(2):
            for y in range(5):
                own = buf[0, z, y]
                before, after = shifted(own, buf[1, z, y])
                for ex, slab in enumerate((before.astype(BF16), own, after.astype(BF16))):
                    for ey in range(3):
                        yc = y - ey
                        if 0 <= yc < 3:
                            r = (ey * 3 + ex) * 64
                            c = (z * 3 + yc) * 128
                            col[r:r + 64, c:c + 128] = slab

    start_halo(cot, cot_s, cot_r, COARSE)

    split[...] = dot(fp_ref[...], pick_ref[...], 1, 0)

    def phase(z, a, b):
        return jnp.concatenate(
            [split[(z * 9 + 3 * yc + a) * 16:(z * 9 + 3 * yc + a) * 16 + 16, b * 128:b * 128 + 128] for yc in range(3)],
            axis=1,
        )

    pooled = []
    for z in range(2):
        window = [jnp.maximum(phase(z, k // 3, k % 3), 0.0) for k in range(9)]
        top = functools.reduce(jnp.maximum, window)
        first = jnp.full(top.shape, 9.0, F32)
        for k in reversed(range(9)):
            first = jnp.where(window[k] == top, float(k), first)
        first = jnp.where(top > 0.0, first, 9.0).astype(BF16)
        for y in range(3):
            fine[0, z + 1, y + 1, 16:32] = first[:, y * 128:y * 128 + 128]
        pooled.append(top.astype(BF16))
    lanes[...] = jnp.zeros_like(lanes)
    for z in range(2):
        for y in range(3):
            c = (z * 3 + y) * 128
            lanes[0, 0:64, c:c + 128] = jnp.maximum(sp_ref[z, y], jnp.zeros((), BF16))
        lanes[1, 64:80, z * 384:z * 384 + 384] = pooled[z]
    split[...] = dot(bi_ref[...], pick_ref[...], 1, 0)

    wait_halo(cot, cot_s, cot_r, COARSE)
    columns(cot)
    third_back = dot(w3_ref[...], col[...], 0, 0)
    for z in range(2):
        for y in range(3):
            c = (z * 3 + y) * 128
            delta[0, z, y + 1] = jnp.where(
                sp_ref[z, y].astype(F32) > 0.0, third_back[:, c:c + 128], 0.0
            ).astype(BF16)
    start_halo(delta, delta_s, delta_r, COARSE)
    grad[...] = jnp.zeros_like(grad)
    grad[0:576] = dot(col[...], lanes[0], 1, 1)
    wait_halo(delta, delta_s, delta_r, COARSE)
    columns(delta)
    pooled_back = dot(w2_ref[...], col[...], 0, 0).astype(BF16)
    for z in range(2):
        for y in range(3):
            c = (z * 3 + y) * 128
            fine[0, z + 1, y + 1, 0:16] = pooled_back[:, c:c + 128]
    start_halo(fine, fine_s, fine_r, FINE)
    grad[0:576] += dot(col[...], lanes[1], 1, 1)
    wait_halo(fine, fine_s, fine_r, FINE)

    for z in range(4):
        own = fine[0, z].reshape(160, 128)
        before, after = shifted(own, fine[1, z].reshape(160, 128))
        own = own.astype(F32)
        views = []
        for src in (before, own, after):
            value = [src[y * 32:y * 32 + 16] for y in range(5)]
            place = [src[y * 32 + 16:y * 32 + 32] for y in range(5)]
            views.append((value, place))
        for ea in range(5):
            a, up = ((2, 0), (0, 1), (1, 1), (2, 1), (0, 2))[ea]
            for eb in range(5):
                b, side = ((2, 0), (0, 1), (1, 1), (2, 1), (0, 2))[eb]
                value, place = views[side]
                for yc in range(3):
                    block = jnp.where(place[yc + up] == float(a * 3 + b), value[yc + up], 0.0)
                    r = (ea * 5 + eb) * 16
                    ext[z, r:r + 16, yc * 128:yc * 128 + 128] = block.astype(BF16)

    first = jnp.zeros((16, 432), F32)
    for z in range(2):
        for a in range(3):
            for b in range(3):
                stack = jnp.concatenate(
                    [
                        ext[z + ez, ((a + ey) * 5 + b) * 16:((a + ey) * 5 + b) * 16 + 48]
                        for ez in range(3) for ey in range(3)
                    ],
                    axis=0,
                )
                back = dot(w1_ref[...], stack, 0, 0).astype(BF16)
                for yc in range(3):
                    r = (z * 9 + 3 * yc + a) * 16
                    gather[r:r + 16, b * 128:b * 128 + 128] = back[:, yc * 128:yc * 128 + 128]
                first = first + dot(phase(z, a, b).astype(BF16), stack, 1, 1)
    for k in range(3):
        grad[576 + k * 16:592 + k * 16] = first[:, k * 128:k * 128 + 128]
    grad[624:640, 0:48] = first[:, 384:432]

    stages = (("gx", gx, 2), ("gz", gz, nz), ("gy", gy, ny))
    offset, length, slot = jnp.int32(0), rows, 0
    done = []
    sends = []
    for axis, at, size in stages:
        share = length // size
        mine = pl.multiple_of(offset + at * share, 8)
        copies = []
        for j in range(1, size):
            peer = lax.rem(at + j, size)
            copy = pltpu.make_async_remote_copy(
                src_ref=grad.at[pl.ds(pl.multiple_of(offset + peer * share, 8), share)],
                dst_ref=inbox.at[slot + j - 1, pl.ds(0, share)],
                send_sem=sum_s.at[slot + j - 1], recv_sem=sum_r.at[slot + j - 1],
                device_id={axis: peer}, device_id_type=MESH,
            )
            copy.start()
            copies.append(copy)
        if axis == "gx":
            result = dot(gather[...], back_ref[...], 1, 0)
            out_ref[...] = result.astype(BF16)
        for copy in copies:
            copy.wait_recv()
        total = grad[pl.ds(mine, share)]
        for j in range(1, size):
            total = total + inbox[slot + j - 1, 0:share]
        grad[pl.ds(mine, share)] = total
        sends += copies
        done.append((axis, at, size, slot))
        slot += size - 1
        offset, length = mine, share
    total_ref[pl.ds(offset, length)] = grad[pl.ds(offset, length)]
    for axis, at, size, slot in reversed(done):
        copies = []
        for j in range(1, size):
            peer = lax.rem(at + j, size)
            copy = pltpu.make_async_remote_copy(
                src_ref=total_ref.at[pl.ds(offset, length)],
                dst_ref=total_ref.at[pl.ds(offset, length)],
                send_sem=all_s.at[slot + j - 1], recv_sem=all_r.at[slot + j - 1],
                device_id={axis: peer}, device_id_type=MESH,
            )
            copy.start()
            copies.append(copy)
        for copy in copies:
            copy.wait_recv()
        sends += copies
        offset = pl.multiple_of(offset - at * length, 8)
        length = length * size
    for copy in sends:
        copy.wait_send()
    wait_sent(cot, cot_s, cot_r, COARSE)
    wait_sent(delta, delta_s, delta_r, COARSE)
    wait_sent(fine, fine_s, fine_r, FINE)


def on_device(
    block_input, first_pre, second_pre, output_cotangent, first_kernel, second_kernel, third_kernel
):
    ny, nz, nx = (lax.axis_size(axis) for axis in ("gy", "gz", "gx"))
    assert nx == 2 and block_input.shape == (12, 2, 9, 384)
    devices = ny * nz * nx
    rows = devices * (-(-640 // (devices * 8)) * 8)

    def fine_rows(x):
        return jnp.pad(x.transpose(1, 2, 0, 3), ((0, 0), (0, 0), (0, 4), (0, 0))).reshape(288, 384)

    def coarse_rows(x):
        return jnp.pad(x.transpose(1, 2, 0, 3), ((0, 0), (0, 0), (0, 4), (0, 0)))

    w1 = jnp.pad(jnp.flip(first_kernel, (0, 1, 2)), ((0, 0),) * 3 + ((0, 4), (0, 4))).reshape(432, 16)
    w2 = jnp.pad(jnp.flip(second_kernel, (0, 1)), ((0, 0),) * 2 + ((0, 4), (0, 4))).reshape(576, 16)
    w3 = jnp.pad(jnp.flip(third_kernel, (0, 1)), ((0, 0),) * 2 + ((0, 4), (0, 4))).reshape(576, 64)
    pick = np.zeros((384, 384), np.float32)
    x = np.arange(384)
    pick[x, (x % 3) * 128 + x // 3] = 1.0
    slots = 1 + (nz - 1) + (ny - 1)
    dma = pltpu.SemaphoreType.DMA
    vmem = pl.BlockSpec(memory_space=pltpu.VMEM)
    out, total = pl.pallas_call(
        functools.partial(kernel, ny, nz, rows),
        out_shape=(
            jax.ShapeDtypeStruct((288, 384), BF16),
            jax.ShapeDtypeStruct((rows, 128), F32),
        ),
        in_specs=[vmem] * 9,
        out_specs=(vmem, vmem),
        scratch_shapes=[
            pltpu.VMEM((2, 2, 5, 64, 128), BF16),
            pltpu.VMEM((2, 2, 5, 64, 128), BF16),
            pltpu.VMEM((2, 4, 5, 32, 128), BF16),
            pltpu.VMEM((576, 768), BF16),
            pltpu.VMEM((4, 400, 384), BF16),
            pltpu.VMEM((288, 384), F32),
            pltpu.VMEM((2, 128, 768), BF16),
            pltpu.VMEM((288, 384), BF16),
            pltpu.VMEM((rows, 128), F32),
            pltpu.VMEM((slots, rows // 2, 128), F32),
            dma((len(COARSE),)), dma((len(COARSE),)),
            dma((len(COARSE),)), dma((len(COARSE),)),
            dma((len(FINE),)), dma((len(FINE),)),
            dma((slots,)), dma((slots,)), dma((slots,)), dma((slots,)),
        ],
        compiler_params=pltpu.CompilerParams(
            collective_id=0, has_side_effects=True, vmem_limit_bytes=48 * 1024 * 1024
        ),
    )(
        fine_rows(block_input), fine_rows(first_pre), coarse_rows(second_pre), coarse_rows(output_cotangent),
        w1, w2, w3, jnp.asarray(pick, BF16), jnp.asarray(pick.T, BF16),
    )
    block_gradient = out.reshape(2, 9, 16, 384)[:, :, :12].transpose(2, 0, 1, 3)
    voxels = 2 * 9 * 384 * devices
    coarse_scale = math.sqrt(voxels // 9)
    fine_scale = math.sqrt(voxels)
    third = jnp.flip(total[:576, :64].reshape(3, 3, 64, 64)[:, :, :60, :60], (0, 1))
    second = jnp.flip(total[:576, 64:80].reshape(3, 3, 64, 16)[:, :, :60, :12], (0, 1))
    first = total[576:640].reshape(4, 16, 128).transpose(0, 2, 1).reshape(512, 16)[:432]
    first = jnp.flip(first.reshape(3, 3, 3, 16, 16)[..., :12, :12], (0, 1, 2))
    return block_gradient, first / fine_scale, second / coarse_scale, third / coarse_scale


def solution(mesh):
    volume = P(None, "gz", ("groups", "gy"), "gx")
    return jax.shard_map(
        on_device,
        mesh=mesh,
        in_specs=(volume,) * 4 + (P(),) * 3,
        out_specs=(
            volume,
            P("groups", None, None, None, None),
            P("groups", None, None, None),
            P("groups", None, None, None),
        ),
        check_vma=False,
    )
```

```python
import functools
import math

import jax
import jax.numpy as jnp
from jax import lax
from jax.experimental import pallas as pl
from jax.experimental.pallas import tpu as pltpu
from jax.sharding import PartitionSpec as P

MESH = pl.DeviceIdType.MESH
F32, BF16 = jnp.float32, jnp.bfloat16


def dot(a, b, da, db):
    return lax.dot_general(a, b, (((da,), (db,)), ((), ())), preferred_element_type=F32)


def neighbour_moves(sections):
    return [(z, y, s) for z in sections for y in (-1, 0, 1) for s in (0, 1) if (z, y, s) != (0, 0, 0)]


COARSE = neighbour_moves((0,))
FINE = neighbour_moves((-1, 0, 1))


class Sum:
    def __init__(self, ny, nz, source, inbox, part, line, total, sems):
        gy, gz, gx = lax.axis_index("gy"), lax.axis_index("gz"), lax.axis_index("gx")
        self.n, self.ny = 2 * nz, ny
        self.share = source.shape[0] // self.n
        self.source, self.inbox, self.part, self.line, self.total = source, inbox, part, line, total
        self.sems, self.me, self.gy = sems, gz * 2 + gx, gy
        self.mine = self.at(self.me)
        self.sent = []

    def at(self, member):
        return pl.ds(pl.multiple_of(member * self.share, 8), self.share)

    def copy(self, kind, j, src, dst, device):
        one = pltpu.make_async_remote_copy(
            src_ref=src, dst_ref=dst, send_sem=self.sems.at[2 * kind, j - 1],
            recv_sem=self.sems.at[2 * kind + 1, j - 1], device_id=device, device_id_type=MESH,
        )
        one.start()
        self.sent.append(one)
        return one

    def member(self, j):
        peer = lax.rem(self.me + j, self.n)
        return peer, {"gz": lax.div(peer, 2), "gx": lax.rem(peer, 2)}

    def scatter(self):
        self.copies = []
        for j in range(1, self.n):
            peer, device = self.member(j)
            self.copies.append(self.copy(0, j, self.source.at[self.at(peer)], self.inbox.at[j - 1], device))

    def exchange(self):
        for one in self.copies:
            one.wait_recv()
        total = self.source[self.mine]
        for j in range(self.n - 1):
            total = total + self.inbox[j]
        self.part[...] = total
        self.copies = [
            self.copy(1, j, self.part, self.line.at[j - 1], {"gy": lax.rem(self.gy + j, self.ny)})
            for j in range(1, self.ny)
        ]

    def gather(self):
        for one in self.copies:
            one.wait_recv()
        total = self.part[...]
        for j in range(self.ny - 1):
            total = total + self.line[j]
        self.total[self.mine] = total
        self.copies = [
            self.copy(2, j, self.total.at[self.mine], self.total.at[self.mine], self.member(j)[1])
            for j in range(1, self.n)
        ]

    def finish(self):
        for one in self.copies:
            one.wait_recv()


def kernel(
    ny, nz, scales,
    bi_ref, fp_ref, sp_ref, oc_ref, k1_ref, k2_ref, k3_ref,
    out_ref, first_ref, second_ref, third_ref,
    cot, delta, fine, col, ext, split, gather, k1, k2, k3, w1, w2, w3,
    sums1, sums2, sums3,
    cot_s, cot_r, delta_s, delta_r, fine_s, fine_r, load,
):
    gy, gz, gx = lax.axis_index("gy"), lax.axis_index("gz"), lax.axis_index("gx")

    def there(z, y):
        ok = None
        for at, step, size in ((gz, z, nz), (gy, y, ny)):
            if step:
                one = at < size - 1 if step > 0 else at > 0
                ok = one if ok is None else jnp.logical_and(ok, one)
        return ok

    def guarded(z, y, run):
        ok = there(z, y)
        if ok is None:
            run()
        else:
            pl.when(ok)(run)

    def device(z, y, s):
        return {"gz": gz + z, "gy": gy + y, "gx": 1 - gx if s else gx}

    loads = [
        pltpu.make_async_copy(src, dst, load.at[at])
        for at, (src, dst) in enumerate(((k1_ref, k1), (k2_ref, k2), (k3_ref, k3)))
    ]
    for one in loads:
        one.start()

    cot[...] = jnp.zeros_like(cot)
    delta[...] = jnp.zeros_like(delta)
    fine[...] = jnp.zeros_like(fine)
    for z in range(2):
        for y in range(3):
            cot[0, z, y + 1] = oc_ref[z, y]

    barrier = pltpu.get_barrier_semaphore()
    count = jnp.int32(0)
    for z, y, s in FINE:
        def greet(z=z, y=y, s=s):
            pl.semaphore_signal(barrier, inc=1, device_id=device(z, y, s), device_id_type=MESH)
        guarded(z, y, greet)
        ok = there(z, y)
        count = count + (1 if ok is None else ok.astype(jnp.int32))
    for j in range(1, 2 * nz):
        peer = lax.rem(gz * 2 + gx + j, 2 * nz)
        pl.semaphore_signal(
            barrier, inc=1, device_id={"gz": lax.div(peer, 2), "gx": lax.rem(peer, 2)}, device_id_type=MESH
        )
    for j in range(1, ny):
        pl.semaphore_signal(barrier, inc=1, device_id={"gy": lax.rem(gy + j, ny)}, device_id_type=MESH)
    pl.semaphore_wait(barrier, count + (2 * nz - 1) + (ny - 1))

    def halo_copy(buf, send, recv, moves, m, arriving=False):
        z, y, s = moves[m]
        zs = slice(0, 2) if buf.shape[1] == 2 else slice(1, 3)
        zd = zs
        if z:
            zs, zd = (slice(2, 3), slice(0, 1)) if z > 0 else (slice(1, 2), slice(3, 4))
        ys = yd = slice(1, 4)
        if y:
            ys, yd = (slice(3, 4), slice(0, 1)) if y > 0 else (slice(1, 2), slice(4, 5))
        return pltpu.make_async_remote_copy(
            src_ref=buf.at[0, zs, ys], dst_ref=buf.at[s, zd, yd],
            send_sem=send.at[m], recv_sem=recv.at[m],
            device_id=device(z, y, s), device_id_type=MESH,
        )

    def start_halo(buf, send, recv, moves):
        for m, (z, y, s) in enumerate(moves):
            guarded(z, y, lambda m=m: halo_copy(buf, send, recv, moves, m).start())

    def wait_halo(buf, send, recv, moves):
        for m, (z, y, s) in enumerate(moves):
            guarded(-z, -y, lambda m=m: halo_copy(buf, send, recv, moves, m).wait_recv())

    def wait_sent(buf, send, recv, moves):
        for m, (z, y, s) in enumerate(moves):
            guarded(z, y, lambda m=m: halo_copy(buf, send, recv, moves, m).wait_send())

    def shifted(own, other):
        own, other = own.astype(F32), other.astype(F32)
        lane = lax.broadcasted_iota(jnp.int32, own.shape, 1)
        left = jnp.where(gx == 1, other, 0.0)
        right = jnp.where(gx == 0, other, 0.0)
        before = pltpu.roll(jnp.where(lane == 127, left, own), 1, 1)
        after = pltpu.roll(jnp.where(lane == 0, right, own), 127, 1)
        return before, after

    def columns(buf):
        for z in range(2):
            for y in range(5):
                own = buf[0, z, y]
                before, after = shifted(own, buf[1, z, y])
                for ex, slab in enumerate((before.astype(BF16), own, after.astype(BF16))):
                    for ey in range(3):
                        yc = y - ey
                        if 0 <= yc < 3:
                            r = (ey * 3 + ex) * 64
                            c = (z * 3 + yc) * 128
                            col[r:r + 64, c:c + 128] = slab

    start_halo(cot, cot_s, cot_r, COARSE)

    row = lax.broadcasted_iota(jnp.int32, (384, 384), 0)
    lane = lax.broadcasted_iota(jnp.int32, (384, 384), 1)
    pick = jnp.where(row == (lane & 127) * 3 + (lane >> 7), 1.0, 0.0).astype(BF16)
    split[...] = dot(fp_ref[...], pick, 1, 0)

    def phase(z, a, b):
        return jnp.concatenate(
            [split[(z * 9 + 3 * yc + a) * 16:(z * 9 + 3 * yc + a) * 16 + 16, b * 128:b * 128 + 128] for yc in range(3)],
            axis=1,
        )

    pooled = []
    for z in range(2):
        window = [jnp.maximum(phase(z, k // 3, k % 3), 0.0) for k in range(9)]
        top = functools.reduce(jnp.maximum, window)
        first = jnp.full(top.shape, 9.0, F32)
        for k in reversed(range(9)):
            first = jnp.where(window[k] == top, float(k), first)
        first = jnp.where(top > 0.0, first, 9.0).astype(BF16)
        for y in range(3):
            fine[0, z + 1, y + 1, 16:32] = first[:, y * 128:y * 128 + 128]
        pooled.append(top.astype(BF16))
    pooled = jnp.concatenate(pooled, axis=1)
    second_relu = jnp.concatenate(
        [jnp.maximum(sp_ref[z, y], jnp.zeros((), BF16)) for z in range(2) for y in range(3)], axis=1
    )
    split[...] = dot(bi_ref[...], pick, 1, 0)

    for one in loads:
        one.wait()
    for w in (w1, w2, w3):
        w[...] = jnp.zeros_like(w)
    unit = jnp.where(
        lax.broadcasted_iota(jnp.int32, (12, 16), 0) == lax.broadcasted_iota(jnp.int32, (12, 16), 1), 1.0, 0.0
    ).astype(BF16)
    for ey in range(3):
        for ex in range(3):
            e = ey * 3 + ex
            w3[e * 64:e * 64 + 60, 0:60] = k3[2 - ey, 2 - ex].astype(F32)
            w2[e * 64:e * 64 + 60] = dot(k2[2 - ey, 2 - ex], unit, 0, 0)
            for ez in range(3):
                r = (ez * 9 + e) * 16
                w1[r:r + 12, 0:12] = k1[2 - ez, 2 - ey, 2 - ex].astype(F32)

    first_sum, second_sum, third_sum = (Sum(ny, nz, *refs) for refs in (sums1, sums2, sums3))
    for one in (first_sum, second_sum, third_sum):
        one.source[...] = jnp.zeros_like(one.source)

    def put(one, value):
        tall, wide = value.shape
        for t in range(-(-wide // 128)):
            part = value[:, t * 128:min(wide, t * 128 + 128)]
            one.source[t * tall:t * tall + tall, 0:part.shape[1]] = part

    def tap(one, tall, e, depth):
        at = e * depth
        block = one.total[at // 128 * tall:at // 128 * tall + tall]
        return block[:, at % 128:at % 128 + depth]

    wait_halo(cot, cot_s, cot_r, COARSE)
    columns(cot)
    third_back = dot(w3[...].astype(BF16), col[...], 0, 0)
    for z in range(2):
        for y in range(3):
            c = (z * 3 + y) * 128
            delta[0, z, y + 1] = jnp.where(
                sp_ref[z, y].astype(F32) > 0.0, third_back[:, c:c + 128], 0.0
            ).astype(BF16)
    start_halo(delta, delta_s, delta_r, COARSE)
    put(third_sum, dot(second_relu, col[...], 1, 1))
    third_sum.scatter()
    wait_halo(delta, delta_s, delta_r, COARSE)
    columns(delta)
    pooled_back = dot(w2[...].astype(BF16), col[...], 0, 0).astype(BF16)
    for z in range(2):
        for y in range(3):
            c = (z * 3 + y) * 128
            fine[0, z + 1, y + 1, 0:16] = pooled_back[:, c:c + 128]
    start_halo(fine, fine_s, fine_r, FINE)
    third_sum.exchange()
    put(second_sum, dot(pooled, col[...], 1, 1))
    second_sum.scatter()
    wait_halo(fine, fine_s, fine_r, FINE)
    third_sum.gather()

    for z in range(4):
        own = fine[0, z].reshape(160, 128)
        before, after = shifted(own, fine[1, z].reshape(160, 128))
        own = own.astype(F32)
        views = []
        for src in (before, own, after):
            value = [src[y * 32:y * 32 + 16] for y in range(5)]
            place = [src[y * 32 + 16:y * 32 + 32] for y in range(5)]
            views.append((value, place))
        for ea in range(5):
            a, up = ((2, 0), (0, 1), (1, 1), (2, 1), (0, 2))[ea]
            for eb in range(5):
                b, side = ((2, 0), (0, 1), (1, 1), (2, 1), (0, 2))[eb]
                value, place = views[side]
                for yc in range(3):
                    block = jnp.where(place[yc + up] == float(a * 3 + b), value[yc + up], 0.0)
                    r = (ea * 5 + eb) * 16
                    ext[z, r:r + 16, yc * 128:yc * 128 + 128] = block.astype(BF16)

    second_sum.exchange()

    def stack(z, a, b):
        return jnp.concatenate(
            [
                ext[z + ez, ((a + ey) * 5 + b) * 16:((a + ey) * 5 + b) * 16 + 48]
                for ez in range(3) for ey in range(3)
            ],
            axis=0,
        )

    places = [(a, b) for a in range(3) for b in range(3)]
    first = jnp.zeros((16, 432), F32)
    for z in range(2):
        for a, b in places:
            first = first + dot(phase(z, a, b).astype(BF16), stack(z, a, b), 1, 1)
    put(first_sum, first)
    first_sum.scatter()
    second_sum.gather()
    weights = w1[...].astype(BF16)
    for z in range(2):
        for a, b in places:
            back = dot(weights, stack(z, a, b), 0, 0).astype(BF16)
            for yc in range(3):
                r = (z * 9 + 3 * yc + a) * 16
                gather[r:r + 16, b * 128:b * 128 + 128] = back[:, yc * 128:yc * 128 + 128]
        if z == 0:
            first_sum.exchange()
    first_sum.gather()
    out_ref[...] = dot(gather[...], pick, 1, 1).astype(BF16)
    first_scale, second_scale, third_scale = scales
    third_sum.finish()
    second_sum.finish()
    for ey in range(3):
        for ex in range(3):
            e = ey * 3 + ex
            second_ref[2 - ey, 2 - ex] = tap(second_sum, 16, e, 64)[0:12, 0:60] * second_scale
    for t in range(5):
        block = third_sum.total[t * 64:t * 64 + 64].T
        for e in range(2 * t, min(2 * t + 2, 9)):
            r = (e - 2 * t) * 64
            third_ref[2 - e // 3, 2 - e % 3] = block[r:r + 60, 0:60] * third_scale
    first_sum.finish()
    for t in range(4):
        block = first_sum.total[t * 16:t * 16 + 16].T
        for e in range(8 * t, min(8 * t + 8, 27)):
            r = (e - 8 * t) * 16
            first_ref[2 - e // 9, 2 - e // 3 % 3, 2 - e % 3] = block[r:r + 12, 0:12] * first_scale
    for one in (first_sum, second_sum, third_sum):
        for copy in one.sent:
            copy.wait_send()
    wait_sent(cot, cot_s, cot_r, COARSE)
    wait_sent(delta, delta_s, delta_r, COARSE)
    wait_sent(fine, fine_s, fine_r, FINE)


def on_device(
    block_input, first_pre, second_pre, output_cotangent, first_kernel, second_kernel, third_kernel
):
    ny, nz, nx = (lax.axis_size(axis) for axis in ("gy", "gz", "gx"))
    assert nx == 2 and block_input.shape == (12, 2, 9, 384)
    devices = ny * nz * nx
    voxels = 2 * 9 * 384 * devices
    coarse_scale = 1.0 / math.sqrt(voxels // 9)
    fine_scale = 1.0 / math.sqrt(voxels)

    def fine_rows(x):
        return jnp.pad(x.transpose(1, 2, 0, 3), ((0, 0), (0, 0), (0, 4), (0, 0))).reshape(288, 384)

    def coarse_rows(x):
        return jnp.pad(x.transpose(1, 2, 0, 3), ((0, 0), (0, 0), (0, 4), (0, 0)))

    dma = pltpu.SemaphoreType.DMA
    vmem = pl.BlockSpec(memory_space=pltpu.VMEM)
    slots = max(2 * nz, ny)

    def sums(rows):
        rows = -(-rows // (16 * nz)) * 16 * nz
        share = rows // (2 * nz)
        return (
            pltpu.VMEM((rows, 128), F32), pltpu.VMEM((2 * nz - 1, share, 128), F32), pltpu.VMEM((share, 128), F32),
            pltpu.VMEM((ny - 1, share, 128), F32), pltpu.VMEM((rows, 128), F32), dma((6, slots)),
        )

    out, first, second, third = pl.pallas_call(
        functools.partial(kernel, ny, nz, (fine_scale, coarse_scale, coarse_scale)),
        out_shape=(
            jax.ShapeDtypeStruct((288, 384), BF16),
            jax.ShapeDtypeStruct((3, 3, 3, 12, 12), F32),
            jax.ShapeDtypeStruct((3, 3, 12, 60), F32),
            jax.ShapeDtypeStruct((3, 3, 60, 60), F32),
        ),
        in_specs=[vmem] * 4 + [pl.BlockSpec(memory_space=pltpu.HBM)] * 3,
        out_specs=(vmem,) * 4,
        scratch_shapes=[
            pltpu.VMEM((2, 2, 5, 64, 128), BF16),
            pltpu.VMEM((2, 2, 5, 64, 128), BF16),
            pltpu.VMEM((2, 4, 5, 32, 128), BF16),
            pltpu.VMEM((576, 768), BF16),
            pltpu.VMEM((4, 400, 384), BF16),
            pltpu.VMEM((288, 384), F32),
            pltpu.VMEM((288, 384), BF16),
            pltpu.VMEM((3, 3, 3, 12, 12), BF16),
            pltpu.VMEM((3, 3, 12, 60), BF16),
            pltpu.VMEM((3, 3, 60, 60), BF16),
            pltpu.VMEM((432, 16), F32),
            pltpu.VMEM((576, 16), F32),
            pltpu.VMEM((576, 64), F32),
            sums(64), sums(80), sums(320),
            dma((len(COARSE),)), dma((len(COARSE),)),
            dma((len(COARSE),)), dma((len(COARSE),)),
            dma((len(FINE),)), dma((len(FINE),)),
            dma((3,)),
        ],
        compiler_params=pltpu.CompilerParams(
            collective_id=0, has_side_effects=True, vmem_limit_bytes=48 * 1024 * 1024
        ),
    )(
        fine_rows(block_input), fine_rows(first_pre), coarse_rows(second_pre), coarse_rows(output_cotangent),
        first_kernel, second_kernel.transpose(0, 1, 3, 2), third_kernel,
    )
    block_gradient = out.reshape(2, 9, 16, 384)[:, :, :12].transpose(2, 0, 1, 3)
    return block_gradient, first, second.transpose(0, 1, 3, 2), third


def solution(mesh):
    volume = P(None, "gz", ("groups", "gy"), "gx")
    return jax.shard_map(
        on_device,
        mesh=mesh,
        in_specs=(volume,) * 4 + (P(),) * 3,
        out_specs=(
            volume,
            P("groups", None, None, None, None),
            P("groups", None, None, None),
            P("groups", None, None, None),
        ),
        check_vma=False,
    )
```
